32 devices in a mesh: chan: 16 (over z, x, core), rows: 2 (over y).
Axes of the slice: x: 2, y: 2, z: 4, core: 2. Of those that a mesh axis runs over, the one named last changes fastest.
Arguments:
- inputs: bfloat16 [1, 2, 256, 2048], P(None, 'rows', None, 'chan'), may hold values from -6 to 6
- weights: bfloat16 [3, 3, 2048, 2048], P(None, None, 'chan'), may hold values from -0.0625 to 0.0625
- cotangent: bfloat16 [1, 2, 256, 2048], P(None, 'rows', None, 'chan'), may hold values from -6 to 6
Outputs:
- outputs: bfloat16 [1, 2, 256, 2048], P(None, 'rows', None, 'chan')
- input_grad: bfloat16 [1, 2, 256, 2048], P(None, 'rows', None, 'chan')
- weight_grad: float32 [3, 3, 2048, 2048], P(None, None, 'chan', 'rows')
The draws below stay inside these ranges and needn't reach their ends.
All inputs are finite; a program needn't handle non-finite values.
Results may differ from the reference program's by a relative error of at most 0.001.
Values may be sent and summed in bfloat16 or wider, within the bound.
A program may use at most 128 MiB of HBM per device.

```python
import jax
import jax.numpy as jnp
from jax import lax

CHANNELS = 2048
WIDTH = 256
BATCH = 1
HEIGHT = 2
PIXELS = 512


def raised(result, own_key, source, target, blocks, factor):
    def block_of(position):
        return (jnp.arange(result.shape[position]) // (result.shape[position] // blocks)).reshape((-1,) + (1,) * (result.ndim - 1 - position))

    first = jax.random.permutation(own_key, blocks)[block_of(target)]
    other_side = (block_of(target) + blocks // 2) % blocks
    return jnp.where((block_of(source) == first) | (block_of(source) == other_side), factor * result, result)


def block_scale(own_key, extent, cuts, least, largest):
    def one(position, parts):
        draws = jax.random.uniform(jax.random.fold_in(jax.random.fold_in(own_key, 6), position), (parts,), jnp.float32, least / len(cuts), largest / len(cuts))
        return jnp.repeat(jnp.exp(draws), extent[position] // parts).reshape((-1,) + (1,) * (len(extent) - position - 1))

    factor_of = one(*cuts[0])
    for cut in cuts[1:]:
        factor_of = factor_of * one(*cut)
    return factor_of


def gaussian(rng, shape, scale, reach, pieces=(), held_as=jnp.bfloat16):
    entries = scale * jax.random.normal(rng, shape, jnp.float32)
    if pieces:
        entries = entries * block_scale(rng, shape, pieces, -0.22, 0.18)
    return jnp.clip(entries, -reach, reach).astype(held_as)


def heavy_noise(stream_key, dims, scale, most, shards, heavy, dtype=jnp.bfloat16):
    values = scale * jax.random.normal(stream_key, dims, jnp.float32)
    if shards:
        values = values * block_scale(stream_key, dims, shards, -0.22, 0.18)
    return jnp.clip(raised(values, jax.random.fold_in(stream_key, 3), *heavy), -most, most).astype(dtype)


def setup_inputs(seed: int = 0) -> dict:
    splits = jax.random.split(jax.random.key(seed), 4)
    return {
        "inputs": gaussian(splits[0], (BATCH, HEIGHT, WIDTH, CHANNELS), 1.0, 6.0, ((1, 2), (3, 16))),
        "weights": heavy_noise(splits[1], (3, 3, CHANNELS, CHANNELS), (9 * CHANNELS) ** -0.5, 0.0625, ((2, 16),), (2, 3, 16, 2.0)),
        "cotangent": heavy_noise(splits[2], (BATCH, HEIGHT, WIDTH, CHANNELS), 1.0, 6.0, ((1, 2), (3, 16)), (1, 3, 2, 2.0)),
    }


def convolve(inputs, weights):
    return lax.conv_general_dilated(inputs, weights, (1, 1), ((1, 1), (1, 1)), dimension_numbers=('NHWC', 'HWIO', 'NHWC'), precision=lax.Precision.HIGHEST)

def reference(inputs, weights, cotangent):
    conv_out, pullback = jax.vjp(convolve, inputs.astype(jnp.float32), weights.astype(jnp.float32))
    data_sum, filter_sum = pullback(cotangent.astype(jnp.float32))
    outputs = conv_out.astype(jnp.bfloat16)
    input_grad = data_sum.astype(jnp.bfloat16)
    weight_grad = filter_sum / jnp.sqrt(jnp.float32(PIXELS))
    return (outputs, input_grad, weight_grad)
```

```python
import jax
import jax.numpy as jnp
from jax import lax
from jax.sharding import PartitionSpec as P


def taps_of(padded, height, breadth):
    return [
        padded[:, ky : ky + height, kx : kx + breadth, :].reshape(-1, padded.shape[3])
        for ky in range(3)
        for kx in range(3)
    ]


def rim(array):
    return jnp.pad(array, ((0, 0), (1, 1), (1, 1), (0, 0)))


def on_device(inputs, weights, cotangent):
    batches, height, breadth, local_ch = inputs.shape
    channels = weights.shape[3]
    groups = lax.axis_size("rows")
    row = lax.axis_index("rows")
    share = channels // groups
    total_pixels = batches * height * groups * breadth

    def around(padded):
        return lax.dynamic_slice_in_dim(padded, row * height, height + 2, axis=1)

    in_padded = rim(lax.all_gather(inputs, "rows", axis=1, tiled=True))
    cot_all = lax.all_gather(
        lax.all_gather(cotangent, "chan", axis=3, tiled=True), "rows", axis=1, tiled=True
    )
    columns = jnp.concatenate(taps_of(around(in_padded), height, breadth), axis=1)
    conv_out = lax.psum_scatter(
        lax.dot_general(
            weights.reshape(9 * local_ch, channels),
            columns,
            (((0,), (1,)), ((), ())),
            preferred_element_type=jnp.float32,
        ),
        "chan",
        scatter_dimension=0,
        tiled=True,
    )
    outputs = conv_out.T.reshape(batches, height, breadth, local_ch).astype(jnp.bfloat16)

    grad_taps = taps_of(around(rim(cot_all)), height, breadth)
    data_sum = 0.0
    for tap in range(9):
        data_sum += lax.dot_general(
            grad_taps[8 - tap],
            weights[tap // 3, tap % 3],
            (((1,), (1,)), ((), ())),
            preferred_element_type=jnp.float32,
        )
    input_grad = data_sum.reshape(batches, height, breadth, local_ch).astype(jnp.bfloat16)

    all_columns = jnp.concatenate(taps_of(in_padded, height * groups, breadth), axis=1)
    mine = lax.dynamic_slice_in_dim(cot_all, row * share, share, axis=3)
    update = lax.dot_general(
        all_columns,
        mine.reshape(total_pixels, share),
        (((0,), (0,)), ((), ())),
        preferred_element_type=jnp.float32,
    )
    weight_grad = (update / jnp.sqrt(jnp.float32(total_pixels))).reshape(3, 3, local_ch, share)
    return (outputs, input_grad, weight_grad)


def solution(mesh):
    in_specs = (
        P(None, "rows", None, "chan"),
        P(None, None, "chan", None),
        P(None, "rows", None, "chan"),
    )
    out_specs = (
        P(None, "rows", None, "chan"),
        P(None, "rows", None, "chan"),
        P(None, None, "chan", "rows"),
    )
    return jax.shard_map(
        on_device, mesh=mesh, in_specs=in_specs, out_specs=out_specs, check_vma=False
    )
```

```python
import functools

import jax
import jax.numpy as jnp
from jax import lax
from jax.experimental import pallas as pl
from jax.experimental.pallas import tpu as pltpu
from jax.sharding import PartitionSpec as P

F32 = jnp.float32
BF16 = jnp.bfloat16
ZS = 4


def moved(value, step):
    rows = value.shape[0]
    rolled = pltpu.roll(value, step % rows, 0)
    at = lax.broadcasted_iota(jnp.int32, value.shape, 0)
    edge = 0 if step == 1 else rows - 1
    return jnp.where(at == edge, 0.0, rolled)


def fused_kernel(
    scale, x_ref, cot_ref, w_hbm, out_ref, igrad_ref, wgrad_hbm,
    w_ref, x_all, cols, cot_all, keep, sib_out, sib_in, x_out, x_in, z_out, z_in, wg,
    in_send, in_recv, cot_send, cot_recv, sib_send, sib_recv, x_send, x_recv,
    z_send, z_recv, w_sem, wg_sem,
):
    chan = lax.axis_index("chan")
    y = lax.axis_index("rows")
    core = chan % 2
    x = (chan // 2) % 2
    z = chan // 4
    deep = x_ref.shape[1]
    channels = w_ref.shape[1]

    def chan_of(zz, xx, cc):
        return zz * 4 + xx * 2 + cc

    def device(ch, row):
        return {"chan": ch, "rows": row}

    sibling = device(chan_of(z, x, 1 - core), y)
    x_peer = device(chan_of(z, 1 - x, core), y)
    y_peer = device(chan, 1 - y)
    z_at = [(z + k) % ZS for k in range(ZS)]
    z_peers = [device(chan_of(z_at[k], x, core), y) for k in range(1, ZS)]

    loads = []
    for part in range(3):
        rows = pl.ds(part * 3 * deep, 3 * deep)
        load = pltpu.make_async_copy(w_hbm.at[rows], w_ref.at[rows], w_sem.at[part])
        load.start()
        loads.append(load)

    barrier = pltpu.get_barrier_semaphore()
    peers = [sibling, x_peer, y_peer] + z_peers
    for peer in peers:
        pl.semaphore_signal(barrier, 1, device_id=peer, device_id_type=pl.DeviceIdType.MESH)
    pl.semaphore_wait(barrier, len(peers))

    pending = []

    def send(src, dst, send_sem, recv_sem, to):
        copy = pltpu.make_async_remote_copy(
            src_ref=src, dst_ref=dst, send_sem=send_sem, recv_sem=recv_sem,
            device_id=to, device_id_type=pl.DeviceIdType.MESH,
        )
        copy.start()
        pending.append(copy)
        return copy

    in_copy = send(x_ref, x_all.at[y], in_send, in_recv.at[y], y_peer)
    x_all[y] = x_ref[...]

    def block(row, ch):
        return cot_all.at[row, :, pl.ds(pl.multiple_of(ch * deep, deep), deep)]

    count = [0]

    def pass_on(src, row, ch, to):
        send(src, block(row, ch), cot_send.at[count[0]], cot_recv.at[row, ch], to)
        count[0] += 1

    def arrived(row, ch):
        pltpu.make_async_remote_copy(
            src_ref=block(row, ch), dst_ref=block(row, ch), send_sem=cot_send.at[0],
            recv_sem=cot_recv.at[row, ch], device_id=sibling,
            device_id_type=pl.DeviceIdType.MESH,
        ).wait_recv()

    for k in (2, 1, 3):
        pass_on(cot_ref, y, chan, z_peers[k - 1])
    pass_on(cot_ref, y, chan, x_peer)
    pass_on(cot_ref, y, chan, y_peer)
    pass_on(cot_ref, y, chan, sibling)
    block(y, chan)[...] = cot_ref[...]

    pltpu.make_async_remote_copy(
        src_ref=x_all.at[1 - y], dst_ref=x_all.at[1 - y], send_sem=in_send,
        recv_sem=in_recv.at[1 - y], device_id=y_peer, device_id_type=pl.DeviceIdType.MESH,
    ).wait_recv()
    for row in range(2):
        line = x_all[row].astype(F32)
        base = row * 3 * deep
        cols[:, base : base + deep] = moved(line, 1).astype(BF16)
        cols[:, base + deep : base + 2 * deep] = x_all[row]
        cols[:, base + 2 * deep : base + 3 * deep] = moved(line, -1).astype(BF16)
    for load in loads:
        load.wait()

    slab = pl.ds(pl.multiple_of((1 - y) * (3 * deep), deep), 6 * deep)

    def conv_chunk(index):
        zz = z_at[(index + 1) % ZS]
        xx = 1 - x if index < ZS else x
        start = pl.multiple_of((zz * 2 + xx) * (2 * deep), 2 * deep)
        part = jnp.dot(cols[...], w_ref[slab, pl.ds(start, 2 * deep)], preferred_element_type=F32)
        low, high = part[:, :deep], part[:, deep:]
        mine = core == 0
        keep[index] = jnp.where(mine, low, high)
        sib_out[index] = jnp.where(mine, high, low)
        return send(sib_out.at[index], sib_in.at[index], sib_send.at[index], sib_recv.at[index], sibling)

    sib_copies = [conv_chunk(i) for i in range(ZS)]

    for k in (1, 3, 2):
        ch = chan_of(z_at[k], x, core)
        arrived(y, ch)
        for to in (x_peer, y_peer, sibling):
            pass_on(block(y, ch), y, ch, to)

    x_copies = []
    for i in range(ZS):
        sib_copies[i].wait_recv()
        x_out[i] = keep[i] + sib_in[i]
        x_copies.append(send(x_out.at[i], x_in.at[i], x_send.at[i], x_recv.at[i], x_peer))

    sib_copies += [conv_chunk(i) for i in range(ZS, 2 * ZS)]

    for k in (0, 1, 3, 2):
        ch = chan_of(z_at[k], 1 - x, core)
        arrived(y, ch)
        for to in (y_peer, sibling):
            pass_on(block(y, ch), y, ch, to)

    z_copies = []
    for i in range(ZS):
        sib_copies[ZS + i].wait_recv()
        x_copies[i].wait_recv()
        z_out[i] = keep[ZS + i] + sib_in[ZS + i] + x_in[i]
        if i < ZS - 1:
            z_copies.append(send(z_out.at[i], z_in.at[i], z_send.at[i], z_recv.at[i], z_peers[i]))

    for xx in (x, 1 - x):
        for k in (0, 1, 3, 2):
            ch = chan_of(z_at[k], xx, core)
            arrived(1 - y, ch)
            pass_on(block(1 - y, ch), 1 - y, ch, sibling)
    for row in (y, 1 - y):
        for xx in (x, 1 - x):
            for k in range(ZS):
                arrived(row, chan_of(z_at[k], xx, 1 - core))

    share = channels // 2
    half = pl.ds(pl.multiple_of(y * share, share), share)
    first = (((0,), (0,)), ((), ()))
    stores = []
    for ky in range(3):
        total = None
        for row in range(2):
            other = row - ky + 1
            if 0 <= other < 2:
                term = lax.dot_general(
                    cols[:, row * 3 * deep : (row + 1) * 3 * deep], cot_all[other, :, half],
                    first, preferred_element_type=F32,
                )
                total = term if total is None else total + term
        rows = pl.ds(ky * 3 * deep, 3 * deep)
        wg[rows] = total * scale
        store = pltpu.make_async_copy(wg.at[rows], wgrad_hbm.at[rows], wg_sem.at[ky])
        store.start()
        stores.append(store)

    second = (((1,), (1,)), ((), ()))
    spread = None
    for row in range(2):
        rows = pl.ds(pl.multiple_of((y - row + 1) * (3 * deep), deep), 3 * deep)
        term = lax.dot_general(cot_all[row], w_ref[rows], second, preferred_element_type=F32)
        spread = term if spread is None else spread + term
    igrad_ref[...] = (
        moved(spread[:, :deep], -1) + spread[:, deep : 2 * deep] + moved(spread[:, 2 * deep :], 1)
    ).astype(BF16)

    total = z_out[ZS - 1]
    for i in range(ZS - 1):
        z_copies[i].wait_recv()
        total = total + z_in[i]
    out_ref[...] = total.astype(BF16)
    for copy in pending:
        copy.wait_send()
    for store in stores:
        store.wait()


def fused(inputs, weights, cotangent):
    breadth, deep = inputs.shape[2:]
    channels = weights.shape[3]
    share = channels // 2
    total_pixels = 2 * breadth
    vmem = pl.BlockSpec(memory_space=pltpu.VMEM)
    hbm = pl.BlockSpec(memory_space=pl.ANY)
    dma = pltpu.SemaphoreType.DMA
    tile = (breadth, deep)
    outs = pl.pallas_call(
        functools.partial(fused_kernel, float(total_pixels) ** -0.5),
        out_shape=[
            jax.ShapeDtypeStruct(tile, BF16),
            jax.ShapeDtypeStruct(tile, BF16),
            jax.ShapeDtypeStruct((9 * deep, share), F32),
        ],
        in_specs=[vmem, vmem, hbm],
        out_specs=[vmem, vmem, hbm],
        scratch_shapes=[
            pltpu.VMEM((9 * deep, channels), BF16),
            pltpu.VMEM((2,) + tile, BF16),
            pltpu.VMEM((breadth, 6 * deep), BF16),
            pltpu.VMEM((2, breadth, channels), BF16),
            pltpu.VMEM((2 * ZS,) + tile, F32),
            pltpu.VMEM((2 * ZS,) + tile, F32),
            pltpu.VMEM((2 * ZS,) + tile, F32),
            pltpu.VMEM((ZS,) + tile, F32),
            pltpu.VMEM((ZS,) + tile, F32),
            pltpu.VMEM((ZS,) + tile, F32),
            pltpu.VMEM((ZS - 1,) + tile, F32),
            pltpu.VMEM((9 * deep, share), F32),
            dma, dma((2,)), dma((31,)), dma((2, 16)), dma((2 * ZS,)), dma((2 * ZS,)),
            dma((ZS,)), dma((ZS,)), dma((ZS - 1,)), dma((ZS - 1,)), dma((3,)), dma((3,)),
        ],
        compiler_params=pltpu.CompilerParams(
            collective_id=0, has_side_effects=True, vmem_limit_bytes=44 * 1024 * 1024
        ),
        cost_estimate=pl.CostEstimate(
            flops=2 * 3 * 9 * deep * channels * breadth,
            bytes_accessed=2 * 9 * deep * channels + 4 * 9 * deep * share,
            transcendentals=0,
        ),
    )(inputs.reshape(tile), cotangent.reshape(tile), weights.reshape(9 * deep, channels))
    return (
        outs[0].reshape(inputs.shape),
        outs[1].reshape(inputs.shape),
        outs[2].reshape(3, 3, deep, share),
    )


def taps_of(padded, height, breadth):
    return [
        padded[:, ky : ky + height, kx : kx + breadth, :].reshape(-1, padded.shape[3])
        for ky in range(3)
        for kx in range(3)
    ]


def rim(array):
    return jnp.pad(array, ((0, 0), (1, 1), (1, 1), (0, 0)))


def on_device(inputs, weights, cotangent):
    batches, height, breadth, local_ch = inputs.shape
    channels = weights.shape[3]
    groups = lax.axis_size("rows")
    if (groups, lax.axis_size("chan"), height, batches) == (2, 16, 1, 1):
        return fused(inputs, weights, cotangent)
    row = lax.axis_index("rows")
    share = channels // groups
    total_pixels = batches * height * groups * breadth

    def around(padded):
        return lax.dynamic_slice_in_dim(padded, row * height, height + 2, axis=1)

    in_padded = rim(lax.all_gather(inputs, "rows", axis=1, tiled=True))
    cot_all = lax.all_gather(
        lax.all_gather(cotangent, "chan", axis=3, tiled=True), "rows", axis=1, tiled=True
    )
    columns = jnp.concatenate(taps_of(around(in_padded), height, breadth), axis=1)
    conv_out = lax.psum_scatter(
        lax.dot_general(
            weights.reshape(9 * local_ch, channels),
            columns,
            (((0,), (1,)), ((), ())),
            preferred_element_type=jnp.float32,
        ),
        "chan",
        scatter_dimension=0,
        tiled=True,
    )
    outputs = conv_out.T.reshape(batches, height, breadth, local_ch).astype(jnp.bfloat16)

    grad_taps = taps_of(around(rim(cot_all)), height, breadth)
    data_sum = 0.0
    for tap in range(9):
        data_sum += lax.dot_general(
            grad_taps[8 - tap],
            weights[tap // 3, tap % 3],
            (((1,), (1,)), ((), ())),
            preferred_element_type=jnp.float32,
        )
    input_grad = data_sum.reshape(batches, height, breadth, local_ch).astype(jnp.bfloat16)

    all_columns = jnp.concatenate(taps_of(in_padded, height * groups, breadth), axis=1)
    mine = lax.dynamic_slice_in_dim(cot_all, row * share, share, axis=3)
    update = lax.dot_general(
        all_columns,
        mine.reshape(total_pixels, share),
        (((0,), (0,)), ((), ())),
        preferred_element_type=jnp.float32,
    )
    weight_grad = (update / jnp.sqrt(jnp.float32(total_pixels))).reshape(3, 3, local_ch, share)
    return (outputs, input_grad, weight_grad)


def solution(mesh):
    in_specs = (
        P(None, "rows", None, "chan"),
        P(None, None, "chan", None),
        P(None, "rows", None, "chan"),
    )
    out_specs = (
        P(None, "rows", None, "chan"),
        P(None, "rows", None, "chan"),
        P(None, None, "chan", "rows"),
    )
    return jax.shard_map(
        on_device, mesh=mesh, in_specs=in_specs, out_specs=out_specs, check_vma=False
    )
```

```python
import functools

import jax
import jax.numpy as jnp
from jax import lax
from jax.experimental import pallas as pl
from jax.experimental.pallas import tpu as pltpu
from jax.sharding import PartitionSpec as P

F32 = jnp.float32
BF16 = jnp.bfloat16
ZS = 4


def moved(value, step):
    rows = value.shape[0]
    rolled = pltpu.roll(value, step % rows, 0)
    at = lax.broadcasted_iota(jnp.int32, value.shape, 0)
    edge = 0 if step == 1 else rows - 1
    return jnp.where(at == edge, 0.0, rolled)


def fused_kernel(
    scale, x_ref, cot_ref, w_hbm, out_ref, igrad_ref, wgrad_hbm,
    w_ref, x_all, cols, cot_all, keep, sib_out, sib_in, x_out, x_in, z_out, z_in, wg,
    in_send, in_recv, cot_send, cot_recv, sib_send, sib_recv, x_send, x_recv,
    z_send, z_recv, w_sem, wg_sem, own_sem,
):
    chan = lax.axis_index("chan")
    y = lax.axis_index("rows")
    core = chan % 2
    x = (chan // 2) % 2
    z = chan // 4
    deep = x_ref.shape[1]
    channels = w_ref.shape[1]

    def block(row, ch):
        return cot_all.at[row, :, pl.ds(pl.multiple_of(ch * deep, deep), deep)]

    own_x = pltpu.make_async_copy(x_ref, x_all.at[y], own_sem.at[0])
    own_x.start()
    own_cot = pltpu.make_async_copy(cot_ref, block(y, chan), own_sem.at[1])
    own_cot.start()

    def chan_of(zz, xx, cc):
        return zz * 4 + xx * 2 + cc

    def device(ch, row):
        return {"chan": ch, "rows": row}

    sibling = device(chan_of(z, x, 1 - core), y)
    x_peer = device(chan_of(z, 1 - x, core), y)
    y_peer = device(chan, 1 - y)
    z_at = [(z + k) % ZS for k in range(ZS)]
    z_peers = [device(chan_of(z_at[k], x, core), y) for k in range(1, ZS)]

    loads = []
    for part in range(3):
        rows = pl.ds(part * 3 * deep, 3 * deep)
        load = pltpu.make_async_copy(w_hbm.at[rows], w_ref.at[rows], w_sem.at[part])
        load.start()
        loads.append(load)

    barrier = pltpu.get_barrier_semaphore()
    peers = [sibling, x_peer, y_peer] + z_peers
    for peer in peers:
        pl.semaphore_signal(barrier, 1, device_id=peer, device_id_type=pl.DeviceIdType.MESH)
    pl.semaphore_wait(barrier, len(peers))

    pending = []

    def send(src, dst, send_sem, recv_sem, to):
        copy = pltpu.make_async_remote_copy(
            src_ref=src, dst_ref=dst, send_sem=send_sem, recv_sem=recv_sem,
            device_id=to, device_id_type=pl.DeviceIdType.MESH,
        )
        copy.start()
        pending.append(copy)
        return copy

    in_copy = send(x_ref, x_all.at[y], in_send, in_recv.at[y], y_peer)

    count = [0]

    def pass_on(src, row, ch, to):
        send(src, block(row, ch), cot_send.at[count[0]], cot_recv.at[row, ch], to)
        count[0] += 1

    def arrived(row, ch):
        pltpu.make_async_remote_copy(
            src_ref=block(row, ch), dst_ref=block(row, ch), send_sem=cot_send.at[0],
            recv_sem=cot_recv.at[row, ch], device_id=sibling,
            device_id_type=pl.DeviceIdType.MESH,
        ).wait_recv()

    for k in (2, 1, 3):
        pass_on(cot_ref, y, chan, z_peers[k - 1])
    pass_on(cot_ref, y, chan, x_peer)
    pass_on(cot_ref, y, chan, y_peer)
    pass_on(cot_ref, y, chan, sibling)
    own_x.wait()
    own_cot.wait()

    pltpu.make_async_remote_copy(
        src_ref=x_all.at[1 - y], dst_ref=x_all.at[1 - y], send_sem=in_send,
        recv_sem=in_recv.at[1 - y], device_id=y_peer, device_id_type=pl.DeviceIdType.MESH,
    ).wait_recv()
    for row in range(2):
        line = x_all[row].astype(F32)
        base = row * 3 * deep
        cols[:, base : base + deep] = moved(line, 1).astype(BF16)
        cols[:, base + deep : base + 2 * deep] = x_all[row]
        cols[:, base + 2 * deep : base + 3 * deep] = moved(line, -1).astype(BF16)
    for load in loads:
        load.wait()

    slab = pl.ds(pl.multiple_of((1 - y) * (3 * deep), deep), 6 * deep)

    def conv_chunk(index):
        zz = z_at[(index + 1) % ZS]
        xx = 1 - x if index < ZS else x
        start = pl.multiple_of((zz * 2 + xx) * (2 * deep), 2 * deep)
        part = jnp.dot(cols[...], w_ref[slab, pl.ds(start, 2 * deep)], preferred_element_type=F32)
        low, high = part[:, :deep], part[:, deep:]
        mine = core == 0
        keep[index] = jnp.where(mine, low, high)
        sib_out[index] = jnp.where(mine, high, low)
        return send(sib_out.at[index], sib_in.at[index], sib_send.at[index], sib_recv.at[index], sibling)

    sib_copies = [conv_chunk(i) for i in range(ZS)]

    for k in (1, 3, 2):
        ch = chan_of(z_at[k], x, core)
        arrived(y, ch)
        for to in (x_peer, y_peer, sibling):
            pass_on(block(y, ch), y, ch, to)

    sib_copies += [conv_chunk(i) for i in range(ZS, 2 * ZS)]

    x_copies = []
    for i in range(ZS):
        sib_copies[i].wait_recv()
        x_out[i] = keep[i] + sib_in[i]
        x_copies.append(send(x_out.at[i], x_in.at[i], x_send.at[i], x_recv.at[i], x_peer))

    for k in (0, 1, 3, 2):
        ch = chan_of(z_at[k], 1 - x, core)
        arrived(y, ch)
        for to in (y_peer, sibling):
            pass_on(block(y, ch), y, ch, to)

    order = [(k, xx) for xx in (x, 1 - x) for k in (0, 1, 3, 2)]
    z_copies = []
    for i in range(ZS):
        for k, xx in order[2 * i : 2 * i + 2]:
            ch = chan_of(z_at[k], xx, core)
            arrived(1 - y, ch)
            pass_on(block(1 - y, ch), 1 - y, ch, sibling)
        sib_copies[ZS + i].wait_recv()
        x_copies[i].wait_recv()
        z_out[i] = keep[ZS + i] + sib_in[ZS + i] + x_in[i]
        if i < ZS - 1:
            z_copies.append(send(z_out.at[i], z_in.at[i], z_send.at[i], z_recv.at[i], z_peers[i]))

    for row in (y, 1 - y):
        for xx in (x, 1 - x):
            for k in range(ZS):
                arrived(row, chan_of(z_at[k], xx, 1 - core))

    share = channels // 2
    half = pl.ds(pl.multiple_of(y * share, share), share)
    first = (((0,), (0,)), ((), ()))
    stores = []
    for ky in range(3):
        total = None
        for row in range(2):
            other = row - ky + 1
            if 0 <= other < 2:
                term = lax.dot_general(
                    cols[:, row * 3 * deep : (row + 1) * 3 * deep], cot_all[other, :, half],
                    first, preferred_element_type=F32,
                )
                total = term if total is None else total + term
        rows = pl.ds(ky * 3 * deep, 3 * deep)
        wg[rows] = total * scale
        store = pltpu.make_async_copy(wg.at[rows], wgrad_hbm.at[rows], wg_sem.at[ky])
        store.start()
        stores.append(store)

    second = (((1,), (1,)), ((), ()))
    spread = None
    for row in range(2):
        rows = pl.ds(pl.multiple_of((y - row + 1) * (3 * deep), deep), 3 * deep)
        term = lax.dot_general(cot_all[row], w_ref[rows], second, preferred_element_type=F32)
        spread = term if spread is None else spread + term
    igrad_ref[...] = (
        moved(spread[:, :deep], -1) + spread[:, deep : 2 * deep] + moved(spread[:, 2 * deep :], 1)
    ).astype(BF16)

    total = z_out[ZS - 1]
    for i in range(ZS - 1):
        z_copies[i].wait_recv()
        total = total + z_in[i]
    out_ref[...] = total.astype(BF16)
    for copy in pending:
        copy.wait_send()
    for store in stores:
        store.wait()


def fused(inputs, weights, cotangent):
    breadth, deep = inputs.shape[2:]
    channels = weights.shape[3]
    share = channels // 2
    total_pixels = 2 * breadth
    vmem = pl.BlockSpec(memory_space=pltpu.VMEM)
    hbm = pl.BlockSpec(memory_space=pltpu.HBM)
    dma = pltpu.SemaphoreType.DMA
    tile = (breadth, deep)
    outs = pl.pallas_call(
        functools.partial(fused_kernel, float(total_pixels) ** -0.5),
        out_shape=[
            jax.ShapeDtypeStruct(tile, BF16),
            jax.ShapeDtypeStruct(tile, BF16),
            jax.ShapeDtypeStruct((9 * deep, share), F32),
        ],
        in_specs=[hbm, hbm, hbm],
        out_specs=[vmem, vmem, hbm],
        scratch_shapes=[
            pltpu.VMEM((9 * deep, channels), BF16),
            pltpu.VMEM((2,) + tile, BF16),
            pltpu.VMEM((breadth, 6 * deep), BF16),
            pltpu.VMEM((2, breadth, channels), BF16),
            pltpu.VMEM((2 * ZS,) + tile, F32),
            pltpu.VMEM((2 * ZS,) + tile, F32),
            pltpu.VMEM((2 * ZS,) + tile, F32),
            pltpu.VMEM((ZS,) + tile, F32),
            pltpu.VMEM((ZS,) + tile, F32),
            pltpu.VMEM((ZS,) + tile, F32),
            pltpu.VMEM((ZS - 1,) + tile, F32),
            pltpu.VMEM((9 * deep, share), F32),
            dma, dma((2,)), dma((31,)), dma((2, 16)), dma((2 * ZS,)), dma((2 * ZS,)),
            dma((ZS,)), dma((ZS,)), dma((ZS - 1,)), dma((ZS - 1,)), dma((3,)), dma((3,)), dma((2,)),
        ],
        compiler_params=pltpu.CompilerParams(
            collective_id=0, has_side_effects=True, vmem_limit_bytes=60 * 1024 * 1024
        ),
        cost_estimate=pl.CostEstimate(
            flops=2 * 3 * 9 * deep * channels * breadth,
            bytes_accessed=2 * 9 * deep * channels + 4 * 9 * deep * share,
            transcendentals=0,
        ),
    )(inputs.reshape(tile), cotangent.reshape(tile), weights.reshape(9 * deep, channels))
    return (
        outs[0].reshape(inputs.shape),
        outs[1].reshape(inputs.shape),
        outs[2].reshape(3, 3, deep, share),
    )


def taps_of(padded, height, breadth):
    return [
        padded[:, ky : ky + height, kx : kx + breadth, :].reshape(-1, padded.shape[3])
        for ky in range(3)
        for kx in range(3)
    ]


def rim(array):
    return jnp.pad(array, ((0, 0), (1, 1), (1, 1), (0, 0)))


def on_device(inputs, weights, cotangent):
    batches, height, breadth, local_ch = inputs.shape
    channels = weights.shape[3]
    groups = lax.axis_size("rows")
    if (groups, lax.axis_size("chan"), height, batches) == (2, 16, 1, 1):
        return fused(inputs, weights, cotangent)
    row = lax.axis_index("rows")
    share = channels // groups
    total_pixels = batches * height * groups * breadth

    def around(padded):
        return lax.dynamic_slice_in_dim(padded, row * height, height + 2, axis=1)

    in_padded = rim(lax.all_gather(inputs, "rows", axis=1, tiled=True))
    cot_all = lax.all_gather(
        lax.all_gather(cotangent, "chan", axis=3, tiled=True), "rows", axis=1, tiled=True
    )
    columns = jnp.concatenate(taps_of(around(in_padded), height, breadth), axis=1)
    conv_out = lax.psum_scatter(
        lax.dot_general(
            weights.reshape(9 * local_ch, channels),
            columns,
            (((0,), (1,)), ((), ())),
            preferred_element_type=jnp.float32,
        ),
        "chan",
        scatter_dimension=0,
        tiled=True,
    )
    outputs = conv_out.T.reshape(batches, height, breadth, local_ch).astype(jnp.bfloat16)

    grad_taps = taps_of(around(rim(cot_all)), height, breadth)
    data_sum = 0.0
    for tap in range(9):
        data_sum += lax.dot_general(
            grad_taps[8 - tap],
            weights[tap // 3, tap % 3],
            (((1,), (1,)), ((), ())),
            preferred_element_type=jnp.float32,
        )
    input_grad = data_sum.reshape(batches, height, breadth, local_ch).astype(jnp.bfloat16)

    all_columns = jnp.concatenate(taps_of(in_padded, height * groups, breadth), axis=1)
    mine = lax.dynamic_slice_in_dim(cot_all, row * share, share, axis=3)
    update = lax.dot_general(
        all_columns,
        mine.reshape(total_pixels, share),
        (((0,), (0,)), ((), ())),
        preferred_element_type=jnp.float32,
    )
    weight_grad = (update / jnp.sqrt(jnp.float32(total_pixels))).reshape(3, 3, local_ch, share)
    return (outputs, input_grad, weight_grad)


def solution(mesh):
    in_specs = (
        P(None, "rows", None, "chan"),
        P(None, None, "chan", None),
        P(None, "rows", None, "chan"),
    )
    out_specs = (
        P(None, "rows", None, "chan"),
        P(None, "rows", None, "chan"),
        P(None, None, "chan", "rows"),
    )
    return jax.shard_map(
        on_device, mesh=mesh, in_specs=in_specs, out_specs=out_specs, check_vma=False
    )
```

```python
import functools

import jax
import jax.numpy as jnp
from jax import lax
from jax.experimental import pallas as pl
from jax.experimental.pallas import tpu as pltpu
from jax.sharding import PartitionSpec as P

F32 = jnp.float32
BF16 = jnp.bfloat16
ZS = 4


def moved(value, step):
    rows = value.shape[0]
    rolled = pltpu.roll(value, step % rows, 0)
    at = lax.broadcasted_iota(jnp.int32, value.shape, 0)
    edge = 0 if step == 1 else rows - 1
    return jnp.where(at == edge, 0.0, rolled)


def fused_kernel(
    x_ref, cot_ref, w_hbm, out_ref, igrad_ref, cols_hbm, half_hbm,
    w_ref, x_all, cols, cot_all, keep, sib_out, sib_in, x_out, x_in, z_out, z_in,
    in_send, in_recv, cot_send, cot_recv, sib_send, sib_recv, x_send, x_recv,
    z_send, z_recv, w_sem, out_sem, own_sem,
):
    chan = lax.axis_index("chan")
    y = lax.axis_index("rows")
    core = chan % 2
    x = (chan // 2) % 2
    z = chan // 4
    deep = x_ref.shape[1]
    channels = w_ref.shape[1]

    def block(row, ch):
        return cot_all.at[row, :, pl.ds(pl.multiple_of(ch * deep, deep), deep)]

    own_x = pltpu.make_async_copy(x_ref, x_all.at[y], own_sem.at[0])
    own_x.start()
    own_cot = pltpu.make_async_copy(cot_ref, block(y, chan), own_sem.at[1])
    own_cot.start()

    def chan_of(zz, xx, cc):
        return zz * 4 + xx * 2 + cc

    def device(ch, row):
        return {"chan": ch, "rows": row}

    sibling = device(chan_of(z, x, 1 - core), y)
    x_peer = device(chan_of(z, 1 - x, core), y)
    y_peer = device(chan, 1 - y)
    z_at = [(z + k) % ZS for k in range(ZS)]
    z_peers = [device(chan_of(z_at[k], x, core), y) for k in range(1, ZS)]

    loads = []
    for part in range(3):
        rows = pl.ds(part * 3 * deep, 3 * deep)
        load = pltpu.make_async_copy(w_hbm.at[rows], w_ref.at[rows], w_sem.at[part])
        load.start()
        loads.append(load)

    barrier = pltpu.get_barrier_semaphore()
    peers = [sibling, x_peer, y_peer] + z_peers
    for peer in peers:
        pl.semaphore_signal(barrier, 1, device_id=peer, device_id_type=pl.DeviceIdType.MESH)
    pl.semaphore_wait(barrier, len(peers))

    pending = []

    def send(src, dst, send_sem, recv_sem, to):
        copy = pltpu.make_async_remote_copy(
            src_ref=src, dst_ref=dst, send_sem=send_sem, recv_sem=recv_sem,
            device_id=to, device_id_type=pl.DeviceIdType.MESH,
        )
        copy.start()
        pending.append(copy)
        return copy

    in_copy = send(x_ref, x_all.at[y], in_send, in_recv.at[y], y_peer)

    count = [0]

    def pass_on(src, row, ch, to):
        send(src, block(row, ch), cot_send.at[count[0]], cot_recv.at[row, ch], to)
        count[0] += 1

    def arrived(row, ch):
        pltpu.make_async_remote_copy(
            src_ref=block(row, ch), dst_ref=block(row, ch), send_sem=cot_send.at[0],
            recv_sem=cot_recv.at[row, ch], device_id=sibling,
            device_id_type=pl.DeviceIdType.MESH,
        ).wait_recv()

    for k in (2, 1, 3):
        pass_on(cot_ref, y, chan, z_peers[k - 1])
    pass_on(cot_ref, y, chan, x_peer)
    pass_on(cot_ref, y, chan, y_peer)
    pass_on(cot_ref, y, chan, sibling)
    own_x.wait()
    own_cot.wait()

    pltpu.make_async_remote_copy(
        src_ref=x_all.at[1 - y], dst_ref=x_all.at[1 - y], send_sem=in_send,
        recv_sem=in_recv.at[1 - y], device_id=y_peer, device_id_type=pl.DeviceIdType.MESH,
    ).wait_recv()
    for row in range(2):
        line = x_all[row].astype(F32)
        base = row * 3 * deep
        cols[:, base : base + deep] = moved(line, 1).astype(BF16)
        cols[:, base + deep : base + 2 * deep] = x_all[row]
        cols[:, base + 2 * deep : base + 3 * deep] = moved(line, -1).astype(BF16)
    kept_cols = pltpu.make_async_copy(cols, cols_hbm, out_sem.at[0])
    kept_cols.start()

    for k in (1, 3, 2):
        ch = chan_of(z_at[k], x, core)
        arrived(y, ch)
        for to in (x_peer, y_peer, sibling):
            pass_on(block(y, ch), y, ch, to)

    for load in loads:
        load.wait()

    slab = pl.ds(pl.multiple_of((1 - y) * (3 * deep), deep), 6 * deep)

    def conv_chunk(index):
        zz = z_at[(index + 1) % ZS]
        xx = 1 - x if index < ZS else x
        start = pl.multiple_of((zz * 2 + xx) * (2 * deep), 2 * deep)
        part = jnp.dot(cols[...], w_ref[slab, pl.ds(start, 2 * deep)], preferred_element_type=F32)
        low, high = part[:, :deep], part[:, deep:]
        mine = core == 0
        keep[index] = jnp.where(mine, low, high)
        sib_out[index] = jnp.where(mine, high, low)
        return send(sib_out.at[index], sib_in.at[index], sib_send.at[index], sib_recv.at[index], sibling)

    sib_copies = [conv_chunk(i) for i in range(ZS)]

    sib_copies += [conv_chunk(i) for i in range(ZS, 2 * ZS)]

    x_copies = []
    for i in range(ZS):
        sib_copies[i].wait_recv()
        x_out[i] = keep[i] + sib_in[i]
        x_copies.append(send(x_out.at[i], x_in.at[i], x_send.at[i], x_recv.at[i], x_peer))

    for k in (0, 1, 3, 2):
        ch = chan_of(z_at[k], 1 - x, core)
        arrived(y, ch)
        for to in (y_peer, sibling):
            pass_on(block(y, ch), y, ch, to)

    order = [(k, xx) for xx in (x, 1 - x) for k in (0, 1, 3, 2)]
    z_copies = []
    for i in range(ZS):
        for k, xx in order[2 * i : 2 * i + 2]:
            ch = chan_of(z_at[k], xx, core)
            arrived(1 - y, ch)
            pass_on(block(1 - y, ch), 1 - y, ch, sibling)
        sib_copies[ZS + i].wait_recv()
        x_copies[i].wait_recv()
        z_out[i] = keep[ZS + i] + sib_in[ZS + i] + x_in[i]
        if i < ZS - 1:
            z_copies.append(send(z_out.at[i], z_in.at[i], z_send.at[i], z_recv.at[i], z_peers[i]))

    for row in (y, 1 - y):
        for xx in (x, 1 - x):
            for k in range(ZS):
                arrived(row, chan_of(z_at[k], xx, 1 - core))

    share = channels // 2
    half = pl.ds(pl.multiple_of(y * share, share), share)
    kept_cot = pltpu.make_async_copy(cot_all.at[:, :, half], half_hbm, out_sem.at[1])
    kept_cot.start()

    second = (((1,), (1,)), ((), ()))
    spread = None
    for row in range(2):
        rows = pl.ds(pl.multiple_of((y - row + 1) * (3 * deep), deep), 3 * deep)
        term = lax.dot_general(cot_all[row], w_ref[rows], second, preferred_element_type=F32)
        spread = term if spread is None else spread + term
    igrad_ref[...] = (
        moved(spread[:, :deep], -1) + spread[:, deep : 2 * deep] + moved(spread[:, 2 * deep :], 1)
    ).astype(BF16)

    total = z_out[ZS - 1]
    for i in range(ZS - 1):
        z_copies[i].wait_recv()
        total = total + z_in[i]
    out_ref[...] = total.astype(BF16)
    for copy in pending:
        copy.wait_send()
    kept_cols.wait()
    kept_cot.wait()


def filter_kernel(
    scale, cols_hbm, half_hbm, conv_hbm, igrad_in, out_hbm, igrad_hbm, wgrad_hbm,
    cols, half, wg, in_sem, through_sem, wg_sem,
):
    wide = cols.shape[1] // 2
    fetch_cols = pltpu.make_async_copy(cols_hbm, cols, in_sem.at[0])
    fetch_cols.start()
    fetch_half = pltpu.make_async_copy(half_hbm, half, in_sem.at[1])
    fetch_half.start()
    copies = [
        pltpu.make_async_copy(conv_hbm, out_hbm, through_sem.at[0]),
        pltpu.make_async_copy(igrad_in, igrad_hbm, through_sem.at[1]),
    ]
    for copy in copies:
        copy.start()
    fetch_cols.wait()
    fetch_half.wait()
    for ky in range(3):
        total = None
        for row in range(2):
            other = row - ky + 1
            if 0 <= other < 2:
                term = lax.dot_general(
                    cols[:, row * wide : (row + 1) * wide], half[other],
                    (((0,), (0,)), ((), ())), preferred_element_type=F32,
                )
                total = term if total is None else total + term
        rows = pl.ds(ky * wide, wide)
        wg[rows] = total * scale
        store = pltpu.make_async_copy(wg.at[rows], wgrad_hbm.at[rows], wg_sem.at[ky])
        store.start()
        copies.append(store)
    for copy in copies:
        copy.wait()


def fused(inputs, weights, cotangent):
    breadth, deep = inputs.shape[2:]
    channels = weights.shape[3]
    share = channels // 2
    total_pixels = 2 * breadth
    vmem = pl.BlockSpec(memory_space=pltpu.VMEM)
    hbm = pl.BlockSpec(memory_space=pltpu.HBM)
    dma = pltpu.SemaphoreType.DMA
    tile = (breadth, deep)
    outs = pl.pallas_call(
        fused_kernel,
        out_shape=[
            jax.ShapeDtypeStruct(tile, BF16),
            jax.ShapeDtypeStruct(tile, BF16),
            jax.ShapeDtypeStruct((breadth, 6 * deep), BF16),
            jax.ShapeDtypeStruct((2, breadth, share), BF16),
        ],
        in_specs=[hbm, hbm, hbm],
        out_specs=[vmem, vmem, hbm, hbm],
        scratch_shapes=[
            pltpu.VMEM((9 * deep, channels), BF16),
            pltpu.VMEM((2,) + tile, BF16),
            pltpu.VMEM((breadth, 6 * deep), BF16),
            pltpu.VMEM((2, breadth, channels), BF16),
            pltpu.VMEM((2 * ZS,) + tile, F32),
            pltpu.VMEM((2 * ZS,) + tile, F32),
            pltpu.VMEM((2 * ZS,) + tile, F32),
            pltpu.VMEM((ZS,) + tile, F32),
            pltpu.VMEM((ZS,) + tile, F32),
            pltpu.VMEM((ZS,) + tile, F32),
            pltpu.VMEM((ZS - 1,) + tile, F32),
            dma, dma((2,)), dma((31,)), dma((2, 16)), dma((2 * ZS,)), dma((2 * ZS,)),
            dma((ZS,)), dma((ZS,)), dma((ZS - 1,)), dma((ZS - 1,)), dma((3,)), dma((2,)), dma((2,)),
        ],
        compiler_params=pltpu.CompilerParams(
            collective_id=0, has_side_effects=True, vmem_limit_bytes=60 * 1024 * 1024
        ),
        cost_estimate=pl.CostEstimate(
            flops=2 * 3 * 9 * deep * channels * breadth,
            bytes_accessed=2 * 9 * deep * channels + 4 * 9 * deep * share,
            transcendentals=0,
        ),
    )(inputs.reshape(tile), cotangent.reshape(tile), weights.reshape(9 * deep, channels))
    outs = pl.pallas_call(
        functools.partial(filter_kernel, float(total_pixels) ** -0.5),
        out_shape=[
            jax.ShapeDtypeStruct(tile, BF16),
            jax.ShapeDtypeStruct(tile, BF16),
            jax.ShapeDtypeStruct((9 * deep, share), F32),
        ],
        in_specs=[hbm] * 4,
        out_specs=[hbm] * 3,
        scratch_shapes=[
            pltpu.VMEM((breadth, 6 * deep), BF16),
            pltpu.VMEM((2, breadth, share), BF16),
            pltpu.VMEM((9 * deep, share), F32),
            dma((2,)), dma((2,)), dma((3,)),
        ],
        compiler_params=pltpu.CompilerParams(vmem_limit_bytes=60 * 1024 * 1024),
    )(outs[2], outs[3], outs[0], outs[1])
    return (
        outs[0].reshape(inputs.shape),
        outs[1].reshape(inputs.shape),
        outs[2].reshape(3, 3, deep, share),
    )


def taps_of(padded, height, breadth):
    return [
        padded[:, ky : ky + height, kx : kx + breadth, :].reshape(-1, padded.shape[3])
        for ky in range(3)
        for kx in range(3)
    ]


def rim(array):
    return jnp.pad(array, ((0, 0), (1, 1), (1, 1), (0, 0)))


def on_device(inputs, weights, cotangent):
    batches, height, breadth, local_ch = inputs.shape
    channels = weights.shape[3]
    groups = lax.axis_size("rows")
    if (groups, lax.axis_size("chan"), height, batches) == (2, 16, 1, 1):
        return fused(inputs, weights, cotangent)
    row = lax.axis_index("rows")
    share = channels // groups
    total_pixels = batches * height * groups * breadth

    def around(padded):
        return lax.dynamic_slice_in_dim(padded, row * height, height + 2, axis=1)

    in_padded = rim(lax.all_gather(inputs, "rows", axis=1, tiled=True))
    cot_all = lax.all_gather(
        lax.all_gather(cotangent, "chan", axis=3, tiled=True), "rows", axis=1, tiled=True
    )
    columns = jnp.concatenate(taps_of(around(in_padded), height, breadth), axis=1)
    conv_out = lax.psum_scatter(
        lax.dot_general(
            weights.reshape(9 * local_ch, channels),
            columns,
            (((0,), (1,)), ((), ())),
            preferred_element_type=jnp.float32,
        ),
        "chan",
        scatter_dimension=0,
        tiled=True,
    )
    outputs = conv_out.T.reshape(batches, height, breadth, local_ch).astype(jnp.bfloat16)

    grad_taps = taps_of(around(rim(cot_all)), height, breadth)
    data_sum = 0.0
    for tap in range(9):
        data_sum += lax.dot_general(
            grad_taps[8 - tap],
            weights[tap // 3, tap % 3],
            (((1,), (1,)), ((), ())),
            preferred_element_type=jnp.float32,
        )
    input_grad = data_sum.reshape(batches, height, breadth, local_ch).astype(jnp.bfloat16)

    all_columns = jnp.concatenate(taps_of(in_padded, height * groups, breadth), axis=1)
    mine = lax.dynamic_slice_in_dim(cot_all, row * share, share, axis=3)
    update = lax.dot_general(
        all_columns,
        mine.reshape(total_pixels, share),
        (((0,), (0,)), ((), ())),
        preferred_element_type=jnp.float32,
    )
    weight_grad = (update / jnp.sqrt(jnp.float32(total_pixels))).reshape(3, 3, local_ch, share)
    return (outputs, input_grad, weight_grad)


def solution(mesh):
    in_specs = (
        P(None, "rows", None, "chan"),
        P(None, None, "chan", None),
        P(None, "rows", None, "chan"),
    )
    out_specs = (
        P(None, "rows", None, "chan"),
        P(None, "rows", None, "chan"),
        P(None, None, "chan", "rows"),
    )
    return jax.shard_map(
        on_device, mesh=mesh, in_specs=in_specs, out_specs=out_specs, check_vma=False
    )
```

```python
import functools

import jax
import jax.numpy as jnp
from jax import lax
from jax.experimental import pallas as pl
from jax.experimental.pallas import tpu as pltpu
from jax.sharding import PartitionSpec as P

F32 = jnp.float32
BF16 = jnp.bfloat16
ZS = 4


def moved(value, step):
    rows = value.shape[0]
    rolled = pltpu.roll(value, step % rows, 0)
    at = lax.broadcasted_iota(jnp.int32, value.shape, 0)
    edge = 0 if step == 1 else rows - 1
    return jnp.where(at == edge, 0.0, rolled)


def fused_kernel(
    x_ref, cot_ref, w_hbm, out_ref, igrad_ref, cols_hbm, half_hbm,
    w_ref, x_all, cols, cot_all, keep, sib_out, sib_in, x_out, x_in, z_out, z_in,
    in_send, in_recv, cot_send, cot_recv, sib_send, sib_recv, x_send, x_recv,
    z_send, z_recv, w_sem, out_sem, own_sem,
):
    chan = lax.axis_index("chan")
    y = lax.axis_index("rows")
    core = chan % 2
    x = (chan // 2) % 2
    z = chan // 4
    deep = x_ref.shape[1]
    channels = w_ref.shape[1]

    def block(row, ch):
        return cot_all.at[row, :, pl.ds(pl.multiple_of(ch * deep, deep), deep)]

    own_x = pltpu.make_async_copy(x_ref, x_all.at[y], own_sem.at[0])
    own_x.start()
    own_cot = pltpu.make_async_copy(cot_ref, block(y, chan), own_sem.at[1])
    own_cot.start()

    def chan_of(zz, xx, cc):
        return zz * 4 + xx * 2 + cc

    def device(ch, row):
        return {"chan": ch, "rows": row}

    sibling = device(chan_of(z, x, 1 - core), y)
    x_peer = device(chan_of(z, 1 - x, core), y)
    y_peer = device(chan, 1 - y)
    z_at = [(z + k) % ZS for k in range(ZS)]
    z_peers = [device(chan_of(z_at[k], x, core), y) for k in range(1, ZS)]

    loads = []
    for part in range(3):
        rows = pl.ds(part * 3 * deep, 3 * deep)
        load = pltpu.make_async_copy(w_hbm.at[rows], w_ref.at[rows], w_sem.at[part])
        load.start()
        loads.append(load)

    barrier = pltpu.get_barrier_semaphore()
    peers = [sibling, x_peer, y_peer] + z_peers
    for peer in peers:
        pl.semaphore_signal(barrier, 1, device_id=peer, device_id_type=pl.DeviceIdType.MESH)
    pl.semaphore_wait(barrier, len(peers))

    pending = []

    def send(src, dst, send_sem, recv_sem, to):
        copy = pltpu.make_async_remote_copy(
            src_ref=src, dst_ref=dst, send_sem=send_sem, recv_sem=recv_sem,
            device_id=to, device_id_type=pl.DeviceIdType.MESH,
        )
        copy.start()
        pending.append(copy)
        return copy

    in_copy = send(x_ref, x_all.at[y], in_send, in_recv.at[y], y_peer)

    count = [0]

    def pass_on(src, row, ch, to):
        send(src, block(row, ch), cot_send.at[count[0]], cot_recv.at[row, ch], to)
        count[0] += 1

    def arrived(row, ch):
        pltpu.make_async_remote_copy(
            src_ref=block(row, ch), dst_ref=block(row, ch), send_sem=cot_send.at[0],
            recv_sem=cot_recv.at[row, ch], device_id=sibling,
            device_id_type=pl.DeviceIdType.MESH,
        ).wait_recv()

    for k in (2, 1, 3):
        pass_on(cot_ref, y, chan, z_peers[k - 1])
    pass_on(cot_ref, y, chan, x_peer)
    pass_on(cot_ref, y, chan, y_peer)
    own_x.wait()
    own_cot.wait()

    pltpu.make_async_remote_copy(
        src_ref=x_all.at[1 - y], dst_ref=x_all.at[1 - y], send_sem=in_send,
        recv_sem=in_recv.at[1 - y], device_id=y_peer, device_id_type=pl.DeviceIdType.MESH,
    ).wait_recv()
    for row in range(2):
        line = x_all[row].astype(F32)
        base = row * 3 * deep
        cols[:, base : base + deep] = moved(line, 1).astype(BF16)
        cols[:, base + deep : base + 2 * deep] = x_all[row]
        cols[:, base + 2 * deep : base + 3 * deep] = moved(line, -1).astype(BF16)
    kept_cols = pltpu.make_async_copy(cols, cols_hbm, out_sem.at[0])
    kept_cols.start()

    for k in (1, 3, 2):
        ch = chan_of(z_at[k], x, core)
        arrived(y, ch)
        for to in (x_peer, y_peer):
            pass_on(block(y, ch), y, ch, to)

    for load in loads:
        load.wait()

    slab = pl.ds(pl.multiple_of((1 - y) * (3 * deep), deep), 6 * deep)

    def conv_chunk(index):
        zz = z_at[(index + 1) % ZS]
        xx = 1 - x if index < ZS else x
        start = pl.multiple_of((zz * 2 + xx) * (2 * deep), 2 * deep)
        part = jnp.dot(cols[...], w_ref[slab, pl.ds(start, 2 * deep)], preferred_element_type=F32)
        low, high = part[:, :deep], part[:, deep:]
        mine = core == 0
        keep[index] = jnp.where(mine, low, high)
        sib_out[index] = jnp.where(mine, high, low)
        return send(sib_out.at[index], sib_in.at[index], sib_send.at[index], sib_recv.at[index], sibling)

    sib_copies = [conv_chunk(i) for i in range(ZS)]

    x_copies = []
    for i in range(ZS):
        sib_copies[i].wait_recv()
        x_out[i] = keep[i] + sib_in[i]
        x_copies.append(send(x_out.at[i], x_in.at[i], x_send.at[i], x_recv.at[i], x_peer))

    sib_copies += [conv_chunk(i) for i in range(ZS, 2 * ZS)]

    for k in range(ZS):
        ch = chan_of(z_at[k], x, core)
        pass_on(block(y, ch), y, ch, sibling)
    for k in (0, 1, 3, 2):
        ch = chan_of(z_at[k], 1 - x, core)
        arrived(y, ch)
        for to in (y_peer, sibling):
            pass_on(block(y, ch), y, ch, to)

    order = [(k, xx) for xx in (x, 1 - x) for k in (0, 1, 3, 2)]
    z_copies = []
    for i in range(ZS):
        for k, xx in order[2 * i : 2 * i + 2]:
            ch = chan_of(z_at[k], xx, core)
            arrived(1 - y, ch)
            pass_on(block(1 - y, ch), 1 - y, ch, sibling)
        sib_copies[ZS + i].wait_recv()
        x_copies[i].wait_recv()
        z_out[i] = keep[ZS + i] + sib_in[ZS + i] + x_in[i]
        if i < ZS - 1:
            z_copies.append(send(z_out.at[i], z_in.at[i], z_send.at[i], z_recv.at[i], z_peers[i]))

    for row in (y, 1 - y):
        for xx in (x, 1 - x):
            for k in range(ZS):
                arrived(row, chan_of(z_at[k], xx, 1 - core))

    share = channels // 2
    half = pl.ds(pl.multiple_of(y * share, share), share)
    kept_cot = pltpu.make_async_copy(cot_all.at[:, :, half], half_hbm, out_sem.at[1])
    kept_cot.start()

    second = (((1,), (1,)), ((), ()))
    spread = None
    for row in range(2):
        rows = pl.ds(pl.multiple_of((y - row + 1) * (3 * deep), deep), 3 * deep)
        term = lax.dot_general(cot_all[row], w_ref[rows], second, preferred_element_type=F32)
        spread = term if spread is None else spread + term
    igrad_ref[...] = (
        moved(spread[:, :deep], -1) + spread[:, deep : 2 * deep] + moved(spread[:, 2 * deep :], 1)
    ).astype(BF16)

    total = z_out[ZS - 1]
    for i in range(ZS - 1):
        z_copies[i].wait_recv()
        total = total + z_in[i]
    out_ref[...] = total.astype(BF16)
    for copy in pending:
        copy.wait_send()
    kept_cols.wait()
    kept_cot.wait()


def filter_kernel(
    scale, cols_hbm, half_hbm, conv_hbm, igrad_in, out_hbm, igrad_hbm, wgrad_hbm,
    cols, half, wg, in_sem, through_sem, wg_sem,
):
    wide = cols.shape[1] // 2
    parts = [pl.ds(row * wide, wide) for row in range(2)]
    fetches = []
    for at, (src, dst) in enumerate(
        [
            (cols_hbm.at[:, parts[0]], cols.at[:, parts[0]]),
            (half_hbm.at[1], half.at[1]),
            (cols_hbm.at[:, parts[1]], cols.at[:, parts[1]]),
            (half_hbm.at[0], half.at[0]),
        ]
    ):
        fetch = pltpu.make_async_copy(src, dst, in_sem.at[at])
        fetch.start()
        fetches.append(fetch)
    copies = [
        pltpu.make_async_copy(conv_hbm, out_hbm, through_sem.at[0]),
        pltpu.make_async_copy(igrad_in, igrad_hbm, through_sem.at[1]),
    ]
    for copy in copies:
        copy.start()
    fetches[0].wait()
    fetches[1].wait()
    piece = wg.shape[1] // 2
    for ky in (0, 2, 1):
        if ky == 2:
            fetches[2].wait()
            fetches[3].wait()
        for side in range(2):
            lanes = pl.ds(side * piece, piece)
            total = None
            for row in range(2):
                other = row - ky + 1
                if 0 <= other < 2:
                    term = lax.dot_general(
                        cols[:, row * wide : (row + 1) * wide], half[other, :, lanes],
                        (((0,), (0,)), ((), ())), preferred_element_type=F32,
                    )
                    total = term if total is None else total + term
            rows = pl.ds(ky * wide, wide)
            wg[rows, lanes] = total * scale
            store = pltpu.make_async_copy(
                wg.at[rows, lanes], wgrad_hbm.at[rows, lanes], wg_sem.at[2 * ky + side]
            )
            store.start()
            copies.append(store)
    for copy in copies:
        copy.wait()


def fused(inputs, weights, cotangent):
    breadth, deep = inputs.shape[2:]
    channels = weights.shape[3]
    share = channels // 2
    total_pixels = 2 * breadth
    vmem = pl.BlockSpec(memory_space=pltpu.VMEM)
    hbm = pl.BlockSpec(memory_space=pltpu.HBM)
    dma = pltpu.SemaphoreType.DMA
    tile = (breadth, deep)
    outs = pl.pallas_call(
        fused_kernel,
        out_shape=[
            jax.ShapeDtypeStruct(tile, BF16),
            jax.ShapeDtypeStruct(tile, BF16),
            jax.ShapeDtypeStruct((breadth, 6 * deep), BF16),
            jax.ShapeDtypeStruct((2, breadth, share), BF16),
        ],
        in_specs=[hbm, hbm, hbm],
        out_specs=[vmem, vmem, hbm, hbm],
        scratch_shapes=[
            pltpu.VMEM((9 * deep, channels), BF16),
            pltpu.VMEM((2,) + tile, BF16),
            pltpu.VMEM((breadth, 6 * deep), BF16),
            pltpu.VMEM((2, breadth, channels), BF16),
            pltpu.VMEM((2 * ZS,) + tile, F32),
            pltpu.VMEM((2 * ZS,) + tile, F32),
            pltpu.VMEM((2 * ZS,) + tile, F32),
            pltpu.VMEM((ZS,) + tile, F32),
            pltpu.VMEM((ZS,) + tile, F32),
            pltpu.VMEM((ZS,) + tile, F32),
            pltpu.VMEM((ZS - 1,) + tile, F32),
            dma, dma((2,)), dma((31,)), dma((2, 16)), dma((2 * ZS,)), dma((2 * ZS,)),
            dma((ZS,)), dma((ZS,)), dma((ZS - 1,)), dma((ZS - 1,)), dma((3,)), dma((2,)), dma((2,)),
        ],
        compiler_params=pltpu.CompilerParams(
            collective_id=0, has_side_effects=True, vmem_limit_bytes=60 * 1024 * 1024
        ),
        cost_estimate=pl.CostEstimate(
            flops=2 * 3 * 9 * deep * channels * breadth,
            bytes_accessed=2 * 9 * deep * channels + 4 * 9 * deep * share,
            transcendentals=0,
        ),
    )(inputs.reshape(tile), cotangent.reshape(tile), weights.reshape(9 * deep, channels))
    outs = pl.pallas_call(
        functools.partial(filter_kernel, float(total_pixels) ** -0.5),
        out_shape=[
            jax.ShapeDtypeStruct(tile, BF16),
            jax.ShapeDtypeStruct(tile, BF16),
            jax.ShapeDtypeStruct((9 * deep, share), F32),
        ],
        in_specs=[hbm] * 4,
        out_specs=[hbm] * 3,
        scratch_shapes=[
            pltpu.VMEM((breadth, 6 * deep), BF16),
            pltpu.VMEM((2, breadth, share), BF16),
            pltpu.VMEM((9 * deep, share), F32),
            dma((4,)), dma((2,)), dma((6,)),
        ],
        compiler_params=pltpu.CompilerParams(vmem_limit_bytes=60 * 1024 * 1024),
    )(outs[2], outs[3], outs[0], outs[1])
    return (
        outs[0].reshape(inputs.shape),
        outs[1].reshape(inputs.shape),
        outs[2].reshape(3, 3, deep, share),
    )


def taps_of(padded, height, breadth):
    return [
        padded[:, ky : ky + height, kx : kx + breadth, :].reshape(-1, padded.shape[3])
        for ky in range(3)
        for kx in range(3)
    ]


def rim(array):
    return jnp.pad(array, ((0, 0), (1, 1), (1, 1), (0, 0)))


def on_device(inputs, weights, cotangent):
    batches, height, breadth, local_ch = inputs.shape
    channels = weights.shape[3]
    groups = lax.axis_size("rows")
    if (groups, lax.axis_size("chan"), height, batches) == (2, 16, 1, 1):
        return fused(inputs, weights, cotangent)
    row = lax.axis_index("rows")
    share = channels // groups
    total_pixels = batches * height * groups * breadth

    def around(padded):
        return lax.dynamic_slice_in_dim(padded, row * height, height + 2, axis=1)

    in_padded = rim(lax.all_gather(inputs, "rows", axis=1, tiled=True))
    cot_all = lax.all_gather(
        lax.all_gather(cotangent, "chan", axis=3, tiled=True), "rows", axis=1, tiled=True
    )
    columns = jnp.concatenate(taps_of(around(in_padded), height, breadth), axis=1)
    conv_out = lax.psum_scatter(
        lax.dot_general(
            weights.reshape(9 * local_ch, channels),
            columns,
            (((0,), (1,)), ((), ())),
            preferred_element_type=jnp.float32,
        ),
        "chan",
        scatter_dimension=0,
        tiled=True,
    )
    outputs = conv_out.T.reshape(batches, height, breadth, local_ch).astype(jnp.bfloat16)

    grad_taps = taps_of(around(rim(cot_all)), height, breadth)
    data_sum = 0.0
    for tap in range(9):
        data_sum += lax.dot_general(
            grad_taps[8 - tap],
            weights[tap // 3, tap % 3],
            (((1,), (1,)), ((), ())),
            preferred_element_type=jnp.float32,
        )
    input_grad = data_sum.reshape(batches, height, breadth, local_ch).astype(jnp.bfloat16)

    all_columns = jnp.concatenate(taps_of(in_padded, height * groups, breadth), axis=1)
    mine = lax.dynamic_slice_in_dim(cot_all, row * share, share, axis=3)
    update = lax.dot_general(
        all_columns,
        mine.reshape(total_pixels, share),
        (((0,), (0,)), ((), ())),
        preferred_element_type=jnp.float32,
    )
    weight_grad = (update / jnp.sqrt(jnp.float32(total_pixels))).reshape(3, 3, local_ch, share)
    return (outputs, input_grad, weight_grad)


def solution(mesh):
    in_specs = (
        P(None, "rows", None, "chan"),
        P(None, None, "chan", None),
        P(None, "rows", None, "chan"),
    )
    out_specs = (
        P(None, "rows", None, "chan"),
        P(None, "rows", None, "chan"),
        P(None, None, "chan", "rows"),
    )
    return jax.shard_map(
        on_device, mesh=mesh, in_specs=in_specs, out_specs=out_specs, check_vma=False
    )
```

```python
import functools

import jax
import jax.numpy as jnp
from jax import lax
from jax.experimental import pallas as pl
from jax.experimental.pallas import tpu as pltpu
from jax.sharding import PartitionSpec as P

F32 = jnp.float32
BF16 = jnp.bfloat16
ZS = 4


def moved(value, step):
    rows = value.shape[0]
    rolled = pltpu.roll(value, step % rows, 0)
    at = lax.broadcasted_iota(jnp.int32, value.shape, 0)
    edge = 0 if step == 1 else rows - 1
    return jnp.where(at == edge, 0.0, rolled)


def fused_kernel(
    x_ref, cot_ref, w_hbm, out_ref, igrad_ref, cols_hbm, half_hbm,
    w_ref, x_all, cols, cols_t, cot_all, keep, sib_out, sib_in, x_out, x_in, z_out, z_in,
    in_send, in_recv, cot_send, cot_recv, sib_send, sib_recv, x_send, x_recv,
    z_send, z_recv, w_sem, out_sem, own_sem,
):
    chan = lax.axis_index("chan")
    y = lax.axis_index("rows")
    core = chan % 2
    x = (chan // 2) % 2
    z = chan // 4
    deep = x_ref.shape[1]
    channels = w_ref.shape[1]

    def block(row, ch):
        return cot_all.at[row, :, pl.ds(pl.multiple_of(ch * deep, deep), deep)]

    own_x = pltpu.make_async_copy(x_ref, x_all.at[y], own_sem.at[0])
    own_x.start()
    own_cot = pltpu.make_async_copy(cot_ref, block(y, chan), own_sem.at[1])
    own_cot.start()

    def chan_of(zz, xx, cc):
        return zz * 4 + xx * 2 + cc

    def device(ch, row):
        return {"chan": ch, "rows": row}

    sibling = device(chan_of(z, x, 1 - core), y)
    x_peer = device(chan_of(z, 1 - x, core), y)
    y_peer = device(chan, 1 - y)
    z_at = [(z + k) % ZS for k in range(ZS)]
    z_peers = [device(chan_of(z_at[k], x, core), y) for k in range(1, ZS)]

    loads = []
    for part in range(3):
        rows = pl.ds(part * 3 * deep, 3 * deep)
        load = pltpu.make_async_copy(w_hbm.at[rows], w_ref.at[rows], w_sem.at[part])
        load.start()
        loads.append(load)

    barrier = pltpu.get_barrier_semaphore()
    peers = [sibling, x_peer, y_peer] + z_peers
    for peer in peers:
        pl.semaphore_signal(barrier, 1, device_id=peer, device_id_type=pl.DeviceIdType.MESH)
    pl.semaphore_wait(barrier, len(peers))

    pending = []

    def send(src, dst, send_sem, recv_sem, to):
        copy = pltpu.make_async_remote_copy(
            src_ref=src, dst_ref=dst, send_sem=send_sem, recv_sem=recv_sem,
            device_id=to, device_id_type=pl.DeviceIdType.MESH,
        )
        copy.start()
        pending.append(copy)
        return copy

    in_copy = send(x_ref, x_all.at[y], in_send, in_recv.at[y], y_peer)

    count = [0]

    def pass_on(src, row, ch, to):
        send(src, block(row, ch), cot_send.at[count[0]], cot_recv.at[row, ch], to)
        count[0] += 1

    def arrived(row, ch):
        pltpu.make_async_remote_copy(
            src_ref=block(row, ch), dst_ref=block(row, ch), send_sem=cot_send.at[0],
            recv_sem=cot_recv.at[row, ch], device_id=sibling,
            device_id_type=pl.DeviceIdType.MESH,
        ).wait_recv()

    for k in (2, 1, 3):
        pass_on(cot_ref, y, chan, z_peers[k - 1])
    pass_on(cot_ref, y, chan, x_peer)
    pass_on(cot_ref, y, chan, y_peer)
    pass_on(cot_ref, y, chan, sibling)
    own_x.wait()
    own_cot.wait()

    pltpu.make_async_remote_copy(
        src_ref=x_all.at[1 - y], dst_ref=x_all.at[1 - y], send_sem=in_send,
        recv_sem=in_recv.at[1 - y], device_id=y_peer, device_id_type=pl.DeviceIdType.MESH,
    ).wait_recv()
    for row in range(2):
        line = x_all[row].astype(F32)
        base = row * 3 * deep
        cols[:, base : base + deep] = moved(line, 1).astype(BF16)
        cols[:, base + deep : base + 2 * deep] = x_all[row]
        cols[:, base + 2 * deep : base + 3 * deep] = moved(line, -1).astype(BF16)

    for k in (1, 3, 2):
        ch = chan_of(z_at[k], x, core)
        arrived(y, ch)
        for to in (x_peer, y_peer, sibling):
            pass_on(block(y, ch), y, ch, to)

    for load in loads:
        load.wait()

    slab = pl.ds(pl.multiple_of((1 - y) * (3 * deep), deep), 6 * deep)

    def conv_chunk(index):
        zz = z_at[(index + 1) % ZS]
        xx = 1 - x if index < ZS else x
        start = pl.multiple_of((zz * 2 + xx) * (2 * deep), 2 * deep)
        part = jnp.dot(cols[...], w_ref[slab, pl.ds(start, 2 * deep)], preferred_element_type=F32)
        low, high = part[:, :deep], part[:, deep:]
        mine = core == 0
        keep[index] = jnp.where(mine, low, high)
        sib_out[index] = jnp.where(mine, high, low)
        return send(sib_out.at[index], sib_in.at[index], sib_send.at[index], sib_recv.at[index], sibling)

    sib_copies = [conv_chunk(i) for i in range(ZS)]

    sib_copies += [conv_chunk(i) for i in range(ZS, 2 * ZS)]

    x_copies = []
    for i in range(ZS):
        sib_copies[i].wait_recv()
        x_out[i] = keep[i] + sib_in[i]
        x_copies.append(send(x_out.at[i], x_in.at[i], x_send.at[i], x_recv.at[i], x_peer))

    for k in (0, 1, 3, 2):
        ch = chan_of(z_at[k], 1 - x, core)
        arrived(y, ch)
        for to in (y_peer, sibling):
            pass_on(block(y, ch), y, ch, to)

    cols_t[...] = cols[...].T
    kept_cols = pltpu.make_async_copy(cols_t, cols_hbm, out_sem.at[0])
    kept_cols.start()

    order = [(k, xx) for xx in (x, 1 - x) for k in (0, 1, 3, 2)]
    z_copies = []
    for i in range(ZS):
        for k, xx in order[2 * i : 2 * i + 2]:
            ch = chan_of(z_at[k], xx, core)
            arrived(1 - y, ch)
            pass_on(block(1 - y, ch), 1 - y, ch, sibling)
        sib_copies[ZS + i].wait_recv()
        x_copies[i].wait_recv()
        z_out[i] = keep[ZS + i] + sib_in[ZS + i] + x_in[i]
        if i < ZS - 1:
            z_copies.append(send(z_out.at[i], z_in.at[i], z_send.at[i], z_recv.at[i], z_peers[i]))

    for row in (y, 1 - y):
        for xx in (x, 1 - x):
            for k in range(ZS):
                arrived(row, chan_of(z_at[k], xx, 1 - core))

    share = channels // 2
    half = pl.ds(pl.multiple_of(y * share, share), share)
    kept_cot = pltpu.make_async_copy(cot_all.at[:, :, half], half_hbm, out_sem.at[1])
    kept_cot.start()

    second = (((1,), (1,)), ((), ()))
    spread = None
    for row in range(2):
        rows = pl.ds(pl.multiple_of((y - row + 1) * (3 * deep), deep), 3 * deep)
        term = lax.dot_general(cot_all[row], w_ref[rows], second, preferred_element_type=F32)
        spread = term if spread is None else spread + term
    igrad_ref[...] = (
        moved(spread[:, :deep], -1) + spread[:, deep : 2 * deep] + moved(spread[:, 2 * deep :], 1)
    ).astype(BF16)

    total = z_out[ZS - 1]
    for i in range(ZS - 1):
        z_copies[i].wait_recv()
        total = total + z_in[i]
    out_ref[...] = total.astype(BF16)
    for copy in pending:
        copy.wait_send()
    kept_cols.wait()
    kept_cot.wait()


def filter_kernel(
    scale, cols_hbm, half_hbm, conv_hbm, igrad_in, out_hbm, igrad_hbm, wgrad_hbm,
    cols, half, wg, in_sem, through_sem, wg_sem,
):
    wide = cols.shape[0] // 2
    fetch_cols = pltpu.make_async_copy(cols_hbm, cols, in_sem.at[0])
    fetch_cols.start()
    fetch_half = pltpu.make_async_copy(half_hbm, half, in_sem.at[1])
    fetch_half.start()
    copies = [
        pltpu.make_async_copy(conv_hbm, out_hbm, through_sem.at[0]),
        pltpu.make_async_copy(igrad_in, igrad_hbm, through_sem.at[1]),
    ]
    for copy in copies:
        copy.start()
    fetch_cols.wait()
    fetch_half.wait()
    for ky in range(3):
        total = None
        for row in range(2):
            other = row - ky + 1
            if 0 <= other < 2:
                term = jnp.dot(
                    cols[row * wide : (row + 1) * wide], half[other],
                    preferred_element_type=F32,
                )
                total = term if total is None else total + term
        rows = pl.ds(ky * wide, wide)
        wg[rows] = total * scale
        store = pltpu.make_async_copy(wg.at[rows], wgrad_hbm.at[rows], wg_sem.at[ky])
        store.start()
        copies.append(store)
    for copy in copies:
        copy.wait()


def fused(inputs, weights, cotangent):
    breadth, deep = inputs.shape[2:]
    channels = weights.shape[3]
    share = channels // 2
    total_pixels = 2 * breadth
    vmem = pl.BlockSpec(memory_space=pltpu.VMEM)
    hbm = pl.BlockSpec(memory_space=pltpu.HBM)
    dma = pltpu.SemaphoreType.DMA
    tile = (breadth, deep)
    outs = pl.pallas_call(
        fused_kernel,
        out_shape=[
            jax.ShapeDtypeStruct(tile, BF16),
            jax.ShapeDtypeStruct(tile, BF16),
            jax.ShapeDtypeStruct((6 * deep, breadth), BF16),
            jax.ShapeDtypeStruct((2, breadth, share), BF16),
        ],
        in_specs=[hbm, hbm, hbm],
        out_specs=[vmem, vmem, hbm, hbm],
        scratch_shapes=[
            pltpu.VMEM((9 * deep, channels), BF16),
            pltpu.VMEM((2,) + tile, BF16),
            pltpu.VMEM((breadth, 6 * deep), BF16),
            pltpu.VMEM((6 * deep, breadth), BF16),
            pltpu.VMEM((2, breadth, channels), BF16),
            pltpu.VMEM((2 * ZS,) + tile, F32),
            pltpu.VMEM((2 * ZS,) + tile, F32),
            pltpu.VMEM((2 * ZS,) + tile, F32),
            pltpu.VMEM((ZS,) + tile, F32),
            pltpu.VMEM((ZS,) + tile, F32),
            pltpu.VMEM((ZS,) + tile, F32),
            pltpu.VMEM((ZS - 1,) + tile, F32),
            dma, dma((2,)), dma((31,)), dma((2, 16)), dma((2 * ZS,)), dma((2 * ZS,)),
            dma((ZS,)), dma((ZS,)), dma((ZS - 1,)), dma((ZS - 1,)), dma((3,)), dma((2,)), dma((2,)),
        ],
        compiler_params=pltpu.CompilerParams(
            collective_id=0, has_side_effects=True, vmem_limit_bytes=60 * 1024 * 1024
        ),
        cost_estimate=pl.CostEstimate(
            flops=2 * 3 * 9 * deep * channels * breadth,
            bytes_accessed=2 * 9 * deep * channels + 4 * 9 * deep * share,
            transcendentals=0,
        ),
    )(inputs.reshape(tile), cotangent.reshape(tile), weights.reshape(9 * deep, channels))
    outs = pl.pallas_call(
        functools.partial(filter_kernel, float(total_pixels) ** -0.5),
        out_shape=[
            jax.ShapeDtypeStruct(tile, BF16),
            jax.ShapeDtypeStruct(tile, BF16),
            jax.ShapeDtypeStruct((9 * deep, share), F32),
        ],
        in_specs=[hbm] * 4,
        out_specs=[hbm] * 3,
        scratch_shapes=[
            pltpu.VMEM((6 * deep, breadth), BF16),
            pltpu.VMEM((2, breadth, share), BF16),
            pltpu.VMEM((9 * deep, share), F32),
            dma((2,)), dma((2,)), dma((3,)),
        ],
        compiler_params=pltpu.CompilerParams(vmem_limit_bytes=60 * 1024 * 1024),
    )(outs[2], outs[3], outs[0], outs[1])
    return (
        outs[0].reshape(inputs.shape),
        outs[1].reshape(inputs.shape),
        outs[2].reshape(3, 3, deep, share),
    )


def taps_of(padded, height, breadth):
    return [
        padded[:, ky : ky + height, kx : kx + breadth, :].reshape(-1, padded.shape[3])
        for ky in range(3)
        for kx in range(3)
    ]


def rim(array):
    return jnp.pad(array, ((0, 0), (1, 1), (1, 1), (0, 0)))


def on_device(inputs, weights, cotangent):
    batches, height, breadth, local_ch = inputs.shape
    channels = weights.shape[3]
    groups = lax.axis_size("rows")
    if (groups, lax.axis_size("chan"), height, batches) == (2, 16, 1, 1):
        return fused(inputs, weights, cotangent)
    row = lax.axis_index("rows")
    share = channels // groups
    total_pixels = batches * height * groups * breadth

    def around(padded):
        return lax.dynamic_slice_in_dim(padded, row * height, height + 2, axis=1)

    in_padded = rim(lax.all_gather(inputs, "rows", axis=1, tiled=True))
    cot_all = lax.all_gather(
        lax.all_gather(cotangent, "chan", axis=3, tiled=True), "rows", axis=1, tiled=True
    )
    columns = jnp.concatenate(taps_of(around(in_padded), height, breadth), axis=1)
    conv_out = lax.psum_scatter(
        lax.dot_general(
            weights.reshape(9 * local_ch, channels),
            columns,
            (((0,), (1,)), ((), ())),
            preferred_element_type=jnp.float32,
        ),
        "chan",
        scatter_dimension=0,
        tiled=True,
    )
    outputs = conv_out.T.reshape(batches, height, breadth, local_ch).astype(jnp.bfloat16)

    grad_taps = taps_of(around(rim(cot_all)), height, breadth)
    data_sum = 0.0
    for tap in range(9):
        data_sum += lax.dot_general(
            grad_taps[8 - tap],
            weights[tap // 3, tap % 3],
            (((1,), (1,)), ((), ())),
            preferred_element_type=jnp.float32,
        )
    input_grad = data_sum.reshape(batches, height, breadth, local_ch).astype(jnp.bfloat16)

    all_columns = jnp.concatenate(taps_of(in_padded, height * groups, breadth), axis=1)
    mine = lax.dynamic_slice_in_dim(cot_all, row * share, share, axis=3)
    update = lax.dot_general(
        all_columns,
        mine.reshape(total_pixels, share),
        (((0,), (0,)), ((), ())),
        preferred_element_type=jnp.float32,
    )
    weight_grad = (update / jnp.sqrt(jnp.float32(total_pixels))).reshape(3, 3, local_ch, share)
    return (outputs, input_grad, weight_grad)


def solution(mesh):
    in_specs = (
        P(None, "rows", None, "chan"),
        P(None, None, "chan", None),
        P(None, "rows", None, "chan"),
    )
    out_specs = (
        P(None, "rows", None, "chan"),
        P(None, "rows", None, "chan"),
        P(None, None, "chan", "rows"),
    )
    return jax.shard_map(
        on_device, mesh=mesh, in_specs=in_specs, out_specs=out_specs, check_vma=False
    )
```
